512 devices in a mesh: blk: 32 (over x_lo, z), uly: 16 (over x_hi, y, core).
Axes of the slice: x: 4 (x_hi: 2, x_lo: 2; x = x_hi * 2 + x_lo), y: 4, z: 16, core: 2. Of those that a mesh axis runs over, the one named last changes fastest.
Arguments:
- query_rows: bfloat16 [4096, 4096], P('blk', 'uly'), may hold values from -6 to 6
- key_rows: bfloat16 [4096, 4096], P('blk', 'uly'), may hold values from -6 to 6
- value_rows: bfloat16 [4096, 4096], P('blk', 'uly'), may hold values from -6 to 6
- output_rows: bfloat16 [4096, 4096], P('blk', 'uly'), may hold values from -1.5 to 1.5
- grad_output: bfloat16 [4096, 4096], P(('blk', 'uly')), may hold values from -96 to 96
- log_norm: float32 [4096, 32], P('blk', 'uly'), may hold values from 7.2 to 9.2
Outputs:
- grad_query: bfloat16 [4096, 4096], P('blk', 'uly')
- grad_key: bfloat16 [4096, 4096], P('blk', 'uly')
- grad_value: bfloat16 [4096, 4096], P('blk', 'uly')
The draws below stay inside these ranges and needn't reach their ends.
All inputs are finite; a program needn't handle non-finite values.
Results may differ from the reference program's by a relative error of at most 0.0056.
Values may be sent and summed in bfloat16 or wider, within the bound.
No kernel may reach another device: no remote copies, remote signals or barrier semaphores. Data moves between devices by JAX's collectives and lax.ppermute only.
A program may use at most 64 MiB of HBM per device.

```python
import math
import jax
import jax.numpy as jnp
from jax import lax

H = 32
HD = 128
D = 4096
SEQ = 4096


def block_scale(rng, shape, cuts, low, top_value):
    def one(dim, shards_of):
        heights = jax.random.uniform(jax.random.fold_in(jax.random.fold_in(rng, 6), dim), (shards_of,), jnp.float32, low / len(cuts), top_value / len(cuts))
        return jnp.repeat(jnp.exp(heights), shape[dim] // shards_of).reshape((-1,) + (1,) * (len(shape) - dim - 1))

    loudness = one(*cuts[0])
    for cut in cuts[1:]:
        loudness = loudness * one(*cut)
    return loudness


def bell_draw(own_key, shape, spread, limit, split=(), held_as=jnp.bfloat16):
    loudness = block_scale(own_key, shape, split, -0.22, 0.18) if split else 1.0
    drawn = jax.random.normal(own_key, shape, jnp.float32) * spread * loudness
    return jnp.minimum(jnp.maximum(drawn, -limit), limit).astype(held_as)


def setup_inputs(seed: int = 0) -> dict:
    keys = jax.random.split(jax.random.key(seed), 7)
    return {
        "query_rows": bell_draw(keys[0], (SEQ, D), 1.0, 6.0, ((0, 32), (1, 16))),
        "key_rows": bell_draw(keys[1], (SEQ, D), 1.0, 6.0, ((0, 32), (1, 16))),
        "value_rows": bell_draw(keys[2], (SEQ, D), 1.0, 6.0, ((0, 32), (1, 16))),
        "output_rows": bell_draw(keys[3], (SEQ, D), 0.25, 1.5, ((0, 32), (1, 16))),
        "grad_output": bell_draw(keys[4], (SEQ, D), 16.0, 96.0, ((0, 512),)),
        "log_norm": jnp.clip(7.2 + 2.0 * jax.random.uniform(keys[5], (SEQ, H), jnp.float32) ** block_scale(keys[5], (SEQ, H), ((0, 32), (1, 16)), -0.2, 0.2), 7.2, 9.2),
    }


def head_grads(pieces):
    query_h, key_h, value_h, dout_h, lnorm_h, delta_h = pieces
    factor = 1.0 / math.sqrt(HD)
    scores = jnp.dot(query_h, key_h.T, preferred_element_type=jnp.float32) * factor
    probs = jnp.exp(scores - lnorm_h[:, None])
    probs_low = probs.astype(jnp.bfloat16)
    dprobs = jnp.dot(dout_h, value_h.T, preferred_element_type=jnp.float32)
    dscore = (probs * (dprobs - delta_h[:, None])).astype(jnp.bfloat16)
    grad_q = jnp.dot(dscore, key_h, preferred_element_type=jnp.float32) * factor
    grad_k = jnp.dot(dscore.T, query_h, preferred_element_type=jnp.float32) * factor
    grad_v = jnp.dot(probs_low.T, dout_h, preferred_element_type=jnp.float32)
    return (grad_q.astype(jnp.bfloat16), grad_k.astype(jnp.bfloat16), grad_v.astype(jnp.bfloat16))

def by_head(rows):
    return rows.reshape(SEQ, H, HD).transpose(1, 0, 2)

def back_rows(grads):
    return grads.transpose(1, 0, 2).reshape(SEQ, H * HD)

def reference(query_rows, key_rows, value_rows, output_rows, grad_output, log_norm):
    product = grad_output.astype(jnp.float32) * output_rows.astype(jnp.float32)
    row_delta = lax.optimization_barrier(jnp.sum(product.reshape(SEQ, H, HD), axis=2))
    pieces = (by_head(query_rows), by_head(key_rows), by_head(value_rows), by_head(grad_output), log_norm.T, row_delta.T)
    grad_q, grad_k, grad_v = lax.map(head_grads, pieces)
    return (back_rows(grad_q), back_rows(grad_k), back_rows(grad_v))
```

```python
import functools
import math

import jax
import jax.numpy as jnp
from jax import lax
from jax.experimental import pallas as pl
from jax.experimental.pallas import tpu as pltpu
from jax.sharding import Mesh, PartitionSpec as P

HD = 128
TOK = 128
ROWS = 2 * TOK
AUX = 16
PAY = 2 * ROWS + AUX
RING = 16
LOG2E = math.log2(math.e)
FACTOR = 1.0 / math.sqrt(HD)
BF = jnp.bfloat16
F32 = jnp.float32
K_STEPS = (1, -1, -2)
Q_STEPS = (4, -4, 8)


def pieces(value):
    high = value.astype(BF)
    rest = value - high.astype(F32)
    mid = rest.astype(BF)
    low = (rest - mid.astype(F32)).astype(BF)
    return [high.astype(F32), mid.astype(F32), low.astype(F32)]


def local(kernel, outs, *args):
    scalars = [pl.BlockSpec(memory_space=pltpu.SMEM)]
    whole = [pl.BlockSpec(memory_space=pltpu.VMEM)]
    return pl.pallas_call(
        kernel,
        out_shape=[jax.ShapeDtypeStruct(shape, dtype) for shape, dtype in outs],
        in_specs=[(scalars if arg.dtype == jnp.int32 else whole)[0] for arg in args],
        out_specs=whole * len(outs),
        compiler_params=pltpu.CompilerParams(vmem_limit_bytes=48 * 1024 * 1024),
    )(*args)


def split_kernel(side, key, value, query, out, lnorm, keep, send):
    def put(mine, other):
        for slot, rows in enumerate((key, value, query, out)):
            at = slice(slot * TOK, (slot + 1) * TOK)
            keep[at, :] = rows[:, mine * HD : (mine + 1) * HD]
            send[at, :] = rows[:, other * HD : (other + 1) * HD]
        for head, dest in ((mine, keep), (other, send)):
            norm = lnorm[head : head + 1, :] * LOG2E
            blank = jnp.zeros((AUX - 3, TOK), F32)
            dest[4 * TOK :, :] = jnp.concatenate(pieces(norm) + [blank], axis=0).astype(BF)

    @pl.when(side[0] == 0)
    def _():
        put(0, 1)

    @pl.when(side[0] != 0)
    def _():
        put(1, 0)


def merge_kernel(side, keep, got, keys, query, out, norm):
    def put(first, second):
        for slot, (dest, at) in enumerate(((keys, 0), (keys, ROWS), (query, 0), (out, 0))):
            rows = slice(slot * TOK, (slot + 1) * TOK)
            dest[at : at + TOK, :] = first[rows, :]
            dest[at + TOK : at + ROWS, :] = second[rows, :]
        norm[:AUX, :] = first[4 * TOK :, :]
        norm[AUX:, :] = second[4 * TOK :, :]

    @pl.when(side[0] == 0)
    def _():
        put(keep, got)

    @pl.when(side[0] != 0)
    def _():
        put(got, keep)


def delta_kernel(query, out, norm, dout, pay):
    pay[:ROWS, :] = query[...]
    pay[ROWS : 2 * ROWS, :] = dout[...]
    product = dout[...].astype(F32) * out[...].astype(F32)
    delta = jnp.sum(product.T, axis=0, keepdims=True)
    first = norm[:AUX, :].astype(F32)
    second = norm[AUX:, :].astype(F32)
    rows = (
        [first[:3, :], second[:3, :]]
        + pieces(delta[:, :TOK])
        + pieces(delta[:, TOK:])
        + [jnp.zeros((AUX - 12, TOK), F32)]
    )
    pay[2 * ROWS :, :] = jnp.concatenate(rows, axis=0).astype(BF)


def dot(left, right, left_dim, right_dim):
    return lax.dot_general(
        left, right, (((left_dim,), (right_dim,)), ((), ())), preferred_element_type=F32
    )


def row_of(aux, at):
    first = aux[at : at + 1, :] + aux[at + 1 : at + 2, :] + aux[at + 2 : at + 3, :]
    second = aux[at + 3 : at + 4, :] + aux[at + 4 : at + 5, :] + aux[at + 5 : at + 6, :]
    return jnp.concatenate([first, second], axis=1)


def tile(pay, keys):
    query = pay[:ROWS, :]
    dout = pay[ROWS : 2 * ROWS, :]
    aux = pay[2 * ROWS :, :].astype(F32)
    key = keys[:ROWS, :]
    value = keys[ROWS:, :]
    probs = jnp.exp2(dot(key, query, 1, 1) * (FACTOR * LOG2E) - row_of(aux, 0))
    dprobs = dot(value, dout, 1, 1)
    dscore = (probs * (dprobs - row_of(aux, 6))).astype(BF)
    grad_v = dot(probs.astype(BF), dout, 1, 0)
    grad_k = dot(dscore, query, 1, 0)
    grad_q = dot(dscore, key, 0, 0)
    return grad_q, grad_k, grad_v


def own_kernel(pay, keys0, keys1, keys2, keys3, grad_q, acc):
    total = None
    for slot, keys in enumerate((keys0, keys1, keys2, keys3)):
        part_q, part_k, part_v = tile(pay, keys)
        total = part_q if total is None else total + part_q
        acc[slot, :ROWS, :] = part_k
        acc[slot, ROWS:, :] = part_v
    grad_q[...] = total * FACTOR


def rest_kernel(pay1, pay2, pay3, keys0, keys1, keys2, keys3, acc, *outs):
    grads_q, grads_kv = outs[:3], outs[3:7]
    pays = (pay1, pay2, pay3)
    totals = [None] * 3
    for slot, keys in enumerate((keys0, keys1, keys2, keys3)):
        sum_k = acc[slot, :ROWS, :]
        sum_v = acc[slot, ROWS:, :]
        for at, pay in enumerate(pays):
            part_q, part_k, part_v = tile(pay, keys)
            totals[at] = part_q if totals[at] is None else totals[at] + part_q
            sum_k += part_k
            sum_v += part_v
        dest = grads_kv[slot]
        dest[:ROWS, :] = (sum_k * FACTOR).astype(dest.dtype)
        dest[ROWS:, :] = sum_v.astype(dest.dtype)
    for at in range(3):
        grads_q[at][...] = (totals[at] * FACTOR).astype(BF)


def sum_kernel(side, own_q, got_q1, got_q2, got_q3, own_kv, got_kv1, got_kv2, got_kv3, keep, send):
    total_q = own_q[...]
    for got in (got_q1, got_q2, got_q3):
        total_q += got[...].astype(F32)
    total_kv = own_kv[...]
    for got in (got_kv1, got_kv2, got_kv3):
        total_kv += got[...].astype(F32)
    total_q = total_q.astype(BF)
    total_kv = total_kv.astype(BF)

    def put(first, second):
        for slot, (rows, at) in enumerate(((total_q, 0), (total_kv, 0), (total_kv, ROWS))):
            dest = slice(slot * TOK, (slot + 1) * TOK)
            first[dest, :] = rows[at : at + TOK, :]
            second[dest, :] = rows[at + TOK : at + ROWS, :]

    @pl.when(side[0] == 0)
    def _():
        put(keep, send)

    @pl.when(side[0] != 0)
    def _():
        put(send, keep)


def join_kernel(side, keep, got, *outs):
    def put(first, second):
        for slot, dest in enumerate(outs):
            rows = slice(slot * TOK, (slot + 1) * TOK)
            dest[:, :HD] = first[rows, :]
            dest[:, HD:] = second[rows, :]

    @pl.when(side[0] == 0)
    def _():
        put(keep, got)

    @pl.when(side[0] != 0)
    def _():
        put(got, keep)


def along(value, steps):
    return lax.ppermute(value, "z", [(at, (at + steps) % RING) for at in range(RING)])


def across(value):
    return lax.ppermute(value, "x_lo", [(0, 1), (1, 0)])


def body(query_rows, key_rows, value_rows, output_rows, grad_output, log_norm):
    side = lax.axis_index("x_lo").astype(jnp.int32).reshape(1)
    heads = grad_output.reshape(8, 16, 2, HD).transpose(2, 1, 0, 3).reshape(32, 8, HD)
    dout = lax.all_to_all(heads, ("x_lo", "x_hi", "y", "core"), 0, 0, tiled=True)
    dout = dout.reshape(ROWS, HD)
    swap = ((4 * TOK + AUX, HD), BF)
    keep, send = local(
        split_kernel,
        [swap, swap],
        side,
        key_rows,
        value_rows,
        query_rows,
        output_rows,
        log_norm.T,
    )
    got = across(send)
    block = ((ROWS, HD), BF)
    pair = ((2 * ROWS, HD), BF)
    keys, query, out, norm = local(
        merge_kernel, [pair, block, block, ((2 * AUX, HD), BF)], side, keep, got
    )
    all_keys = [keys] + [along(keys, step) for step in K_STEPS]
    (pay,) = local(delta_kernel, [((PAY, HD), BF)], query, out, norm, dout)
    pays = [along(pay, step) for step in Q_STEPS]
    own_q, acc = local(
        own_kernel, [((ROWS, HD), F32), ((4, 2 * ROWS, HD), F32)], pay, *all_keys
    )
    outs = local(
        rest_kernel,
        [block] * 3 + [((2 * ROWS, HD), F32)] + [pair] * 3,
        *pays,
        *all_keys,
        acc,
    )
    got_q = [along(part, -step) for part, step in zip(outs[:3], Q_STEPS)]
    got_kv = [along(part, -step) for part, step in zip(outs[4:], K_STEPS)]
    half = ((3 * TOK, HD), BF)
    keep, send = local(sum_kernel, [half, half], side, own_q, *got_q, outs[3], *got_kv)
    got = across(send)
    return tuple(local(join_kernel, [((TOK, 2 * HD), BF)] * 3, side, keep, got))


def solution(mesh):
    fine = Mesh(
        mesh.devices.reshape(2, RING, 2, 4, 2), ("x_lo", "z", "x_hi", "y", "core")
    )
    blk, uly = ("x_lo", "z"), ("x_hi", "y", "core")
    placed = P(blk, uly)
    return jax.shard_map(
        body,
        mesh=fine,
        in_specs=(placed, placed, placed, placed, P(blk + uly, None), placed),
        out_specs=(placed, placed, placed),
        check_vma=False,
    )
```

```python
import functools
import math

import jax
import jax.numpy as jnp
from jax import lax
from jax.experimental import pallas as pl
from jax.experimental.pallas import tpu as pltpu
from jax.sharding import Mesh, PartitionSpec as P

HD = 128
TOK = 128
ROWS = 2 * TOK
AUX = 16
PAY = 2 * ROWS + AUX
RING = 16
LOG2E = math.log2(math.e)
FACTOR = 1.0 / math.sqrt(HD)
BF = jnp.bfloat16
F32 = jnp.float32
K_STEPS = (1, -1, -2)
GROUP = 4


def pieces(value):
    high = value.astype(BF)
    rest = value - high.astype(F32)
    mid = rest.astype(BF)
    low = (rest - mid.astype(F32)).astype(BF)
    return [high.astype(F32), mid.astype(F32), low.astype(F32)]


def local(kernel, outs, *args, far=(), scratch=()):
    scalars = [pl.BlockSpec(memory_space=pltpu.SMEM)]
    whole = [pl.BlockSpec(memory_space=pltpu.VMEM)]
    return pl.pallas_call(
        kernel,
        out_shape=[jax.ShapeDtypeStruct(shape, dtype) for shape, dtype in outs],
        in_specs=[
            pl.BlockSpec(memory_space=pltpu.HBM)
            if at in far
            else (scalars if arg.dtype == jnp.int32 else whole)[0]
            for at, arg in enumerate(args)
        ],
        out_specs=whole * len(outs),
        scratch_shapes=list(scratch),
        compiler_params=pltpu.CompilerParams(vmem_limit_bytes=48 * 1024 * 1024),
    )(*args)


def split_kernel(
    side, dout, key, value, query, out, lnorm, heads, keep, send, dout_in, rows_in, dout_sem, rows_sem
):
    load = pltpu.make_async_copy(dout, dout_in, dout_sem)
    load.start()
    loads = []
    for slot, rows in enumerate((key, value, query, out)):
        loads.append(pltpu.make_async_copy(rows, rows_in.at[slot], rows_sem.at[slot]))
        loads[-1].start()
    load.wait()
    for head in range(32):
        heads[(head % 2) * 16 + head // 2] = dout_in[:, head * HD : (head + 1) * HD]
    for each in loads:
        each.wait()

    def put(mine, other):
        for slot in range(4):
            at = slice(slot * TOK, (slot + 1) * TOK)
            keep[at, :] = rows_in[slot, :, mine * HD : (mine + 1) * HD]
            send[at, :] = rows_in[slot, :, other * HD : (other + 1) * HD]
        for head, dest in ((mine, keep), (other, send)):
            norm = lnorm[head : head + 1, :] * LOG2E
            blank = jnp.zeros((AUX - 3, TOK), F32)
            dest[4 * TOK :, :] = jnp.concatenate(pieces(norm) + [blank], axis=0).astype(BF)

    @pl.when(side[0] == 0)
    def _():
        put(0, 1)

    @pl.when(side[0] != 0)
    def _():
        put(1, 0)


def merge_kernel(side, keep, got, keys, query, out, norm):
    def put(first, second):
        for slot, (dest, at) in enumerate(((keys, 0), (keys, ROWS), (query, 0), (out, 0))):
            rows = slice(slot * TOK, (slot + 1) * TOK)
            dest[at : at + TOK, :] = first[rows, :]
            dest[at + TOK : at + ROWS, :] = second[rows, :]
        norm[:AUX, :] = first[4 * TOK :, :]
        norm[AUX:, :] = second[4 * TOK :, :]

    @pl.when(side[0] == 0)
    def _():
        put(keep, got)

    @pl.when(side[0] != 0)
    def _():
        put(got, keep)


def delta_kernel(query, out, norm, dout, pay):
    pay[:ROWS, :] = query[...]
    pay[ROWS : 2 * ROWS, :] = dout[...]
    product = dout[...].astype(F32) * out[...].astype(F32)
    delta = jnp.sum(product.T, axis=0, keepdims=True)
    first = norm[:AUX, :].astype(F32)
    second = norm[AUX:, :].astype(F32)
    rows = (
        [first[:3, :], second[:3, :]]
        + pieces(delta[:, :TOK])
        + pieces(delta[:, TOK:])
        + [jnp.zeros((AUX - 12, TOK), F32)]
    )
    pay[2 * ROWS :, :] = jnp.concatenate(rows, axis=0).astype(BF)


def dot(left, right, left_dim, right_dim):
    return lax.dot_general(
        left, right, (((left_dim,), (right_dim,)), ((), ())), preferred_element_type=F32
    )


def row_of(aux, at):
    first = aux[at : at + 1, :] + aux[at + 1 : at + 2, :] + aux[at + 2 : at + 3, :]
    second = aux[at + 3 : at + 4, :] + aux[at + 4 : at + 5, :] + aux[at + 5 : at + 6, :]
    return jnp.concatenate([first, second], axis=1)


def tile(pay, keys):
    query = pay[:ROWS, :]
    dout = pay[ROWS : 2 * ROWS, :]
    aux = pay[2 * ROWS :, :].astype(F32)
    probs = jnp.exp2(dot(keys[:ROWS, :], query, 1, 1) * (FACTOR * LOG2E) - row_of(aux, 0))
    dprobs = dot(keys[ROWS:, :], dout, 1, 1)
    dscore = (probs * (dprobs - row_of(aux, 6))).astype(BF)
    grad_v = dot(probs.astype(BF), dout, 1, 0)
    grad_k = dot(dscore, query, 1, 0)
    return dscore, grad_k, grad_v


def pairs_kernel(pays, keys0, keys1, keys2, keys3, dscores, *grads_kv):
    for slot, keys in enumerate((keys0, keys1, keys2, keys3)):
        sum_k = sum_v = None
        for at in range(GROUP):
            dscore, part_k, part_v = tile(pays.at[at], keys)
            dscores[at, slot * ROWS : (slot + 1) * ROWS, :] = dscore
            sum_k = part_k if at == 0 else sum_k + part_k
            sum_v = part_v if at == 0 else sum_v + part_v
        dest = grads_kv[slot]
        dest[:ROWS, :] = (sum_k * FACTOR).astype(dest.dtype)
        dest[ROWS:, :] = sum_v.astype(dest.dtype)


def query_kernel(dscores, keys0, keys1, keys2, keys3, grads_q):
    for at in range(GROUP):
        total = None
        for slot, keys in enumerate((keys0, keys1, keys2, keys3)):
            part = dot(keys[:ROWS, :], dscores[at, slot * ROWS : (slot + 1) * ROWS, :], 0, 0)
            total = part if slot == 0 else total + part
        grads_q[at] = (total * FACTOR).astype(BF)


def sum_kernel(side, got_q, own, got1, got2, got3, keep, send):
    total_q = got_q[0].astype(F32)
    for at in range(1, GROUP):
        total_q += got_q[at].astype(F32)
    total_q = total_q.T.astype(BF)
    total = own[...]
    for got in (got1, got2, got3):
        total += got[...].astype(F32)
    total = total.astype(BF)

    def put(first, second):
        for slot, (rows, at) in enumerate(((total_q, 0), (total, 0), (total, ROWS))):
            dest = slice(slot * TOK, (slot + 1) * TOK)
            first[dest, :] = rows[at : at + TOK, :]
            second[dest, :] = rows[at + TOK : at + ROWS, :]

    @pl.when(side[0] == 0)
    def _():
        put(keep, send)

    @pl.when(side[0] != 0)
    def _():
        put(send, keep)


def join_kernel(side, keep, got, *outs):
    def put(first, second):
        for slot, dest in enumerate(outs):
            rows = slice(slot * TOK, (slot + 1) * TOK)
            dest[:, :HD] = first[rows, :]
            dest[:, HD:] = second[rows, :]

    @pl.when(side[0] == 0)
    def _():
        put(keep, got)

    @pl.when(side[0] != 0)
    def _():
        put(got, keep)


def along(value, steps):
    pairs = []
    for at in range(RING):
        for core, shift in enumerate((steps, -steps)):
            pairs.append((2 * at + core, 2 * ((at + shift) % RING) + core))
    return lax.ppermute(value, ("z_hi", "z_lo", "core"), pairs)


def across(value):
    return lax.ppermute(value, "x_lo", [(0, 1), (1, 0)])


def body(query_rows, key_rows, value_rows, output_rows, grad_output, log_norm):
    side = lax.axis_index("x_lo").astype(jnp.int32).reshape(1)
    swap = ((4 * TOK + AUX, HD), BF)
    heads, keep, send = local(
        split_kernel,
        [((32, 8, HD), BF), swap, swap],
        side,
        *[
            pltpu.with_memory_space_constraint(rows, pltpu.HBM)
            for rows in (grad_output, key_rows, value_rows, query_rows, output_rows)
        ],
        log_norm.T,
        far=range(1, 6),
        scratch=(
            pltpu.VMEM((8, 32 * HD), BF),
            pltpu.VMEM((4, TOK, 2 * HD), BF),
            pltpu.SemaphoreType.DMA,
            pltpu.SemaphoreType.DMA((4,)),
        ),
    )
    dout = lax.all_to_all(heads, ("x_lo", "x_hi", "y", "core"), 0, 0, tiled=True)
    dout = dout.reshape(ROWS, HD)
    got = across(send)
    block = ((ROWS, HD), BF)
    pair = ((2 * ROWS, HD), BF)
    keys, query, out, norm = local(
        merge_kernel, [pair, block, block, ((2 * AUX, HD), BF)], side, keep, got
    )
    all_keys = [keys] + [along(keys, step) for step in K_STEPS]
    (pay,) = local(delta_kernel, [((PAY, HD), BF)], query, out, norm, dout)
    pays = lax.all_gather(pay, "z_hi")
    outs = local(
        pairs_kernel,
        [((GROUP, 4 * ROWS, ROWS), BF), ((2 * ROWS, HD), F32)] + [pair] * 3,
        pays,
        *all_keys,
    )
    got_kv = [along(part, -step) for part, step in zip(outs[2:], K_STEPS)]
    (parts_q,) = local(query_kernel, [((GROUP, HD, ROWS), BF)], outs[0], *all_keys)
    got_q = lax.all_to_all(parts_q, "z_hi", 0, 0, tiled=True)
    got_kv = [along(part, -step) for part, step in zip(outs[2:], K_STEPS)]
    half = ((3 * TOK, HD), BF)
    keep, send = local(sum_kernel, [half, half], side, got_q, outs[1], *got_kv)
    got = across(send)
    return tuple(local(join_kernel, [((TOK, 2 * HD), BF)] * 3, side, keep, got))


def solution(mesh):
    fine = Mesh(
        mesh.devices.reshape(2, 4, 4, 2, 4, 2), ("x_lo", "z_hi", "z_lo", "x_hi", "y", "core")
    )
    blk, uly = ("x_lo", "z_hi", "z_lo"), ("x_hi", "y", "core")
    placed = P(blk, uly)
    return jax.shard_map(
        body,
        mesh=fine,
        in_specs=(placed, placed, placed, placed, P(blk + uly, None), placed),
        out_specs=(placed, placed, placed),
        check_vma=False,
    )
```

```python
import functools
import math

import jax
import jax.numpy as jnp
from jax import lax
from jax.experimental import pallas as pl
from jax.experimental.pallas import tpu as pltpu
from jax.sharding import Mesh, PartitionSpec as P

HD = 128
TOK = 128
ROWS = 2 * TOK
AUX = 16
PAY = 2 * ROWS + AUX
RING = 16
LOG2E = math.log2(math.e)
FACTOR = 1.0 / math.sqrt(HD)
BF = jnp.bfloat16
F32 = jnp.float32
KEYS = 4 * ROWS
CHUNK = 512
LONG = pl.CostEstimate(flops=10**11, bytes_accessed=10**8, transcendentals=0)
K_STEPS = (1, -1, -2)
GROUP = 4


def pieces(value):
    high = value.astype(BF)
    rest = value - high.astype(F32)
    mid = rest.astype(BF)
    low = (rest - mid.astype(F32)).astype(BF)
    return [high.astype(F32), mid.astype(F32), low.astype(F32)]


def local(kernel, outs, *args, far=(), scratch=(), cost=None):
    scalars = [pl.BlockSpec(memory_space=pltpu.SMEM)]
    whole = [pl.BlockSpec(memory_space=pltpu.VMEM)]
    return pl.pallas_call(
        kernel,
        out_shape=[jax.ShapeDtypeStruct(shape, dtype) for shape, dtype in outs],
        in_specs=[
            pl.BlockSpec(memory_space=pltpu.HBM)
            if at in far
            else (scalars if arg.dtype == jnp.int32 else whole)[0]
            for at, arg in enumerate(args)
        ],
        out_specs=whole * len(outs),
        scratch_shapes=list(scratch),
        cost_estimate=cost,
        compiler_params=pltpu.CompilerParams(vmem_limit_bytes=48 * 1024 * 1024),
    )(*args)


def split_kernel(
    side, dout, key, value, query, out, lnorm, heads, keep, send, dout_in, rows_in, norm_in, dout_sem, rows_sem, norm_sem
):
    load = pltpu.make_async_copy(dout, dout_in, dout_sem)
    load.start()
    norm_load = pltpu.make_async_copy(lnorm, norm_in, norm_sem)
    norm_load.start()
    loads = []
    for slot, rows in enumerate((key, value, query, out)):
        loads.append(pltpu.make_async_copy(rows, rows_in.at[slot], rows_sem.at[slot]))
        loads[-1].start()
    load.wait()
    for head in range(32):
        heads[(head % 2) * 16 + head // 2] = dout_in[:, head * HD : (head + 1) * HD]
    for each in loads:
        each.wait()
    norm_load.wait()

    def put(mine, other):
        for slot in range(4):
            at = slice(slot * TOK, (slot + 1) * TOK)
            keep[at, :] = rows_in[slot, :, mine * HD : (mine + 1) * HD]
            send[at, :] = rows_in[slot, :, other * HD : (other + 1) * HD]
        for head, dest in ((mine, keep), (other, send)):
            norm = norm_in[head : head + 1, :] * LOG2E
            blank = jnp.zeros((AUX - 3, TOK), F32)
            dest[4 * TOK :, :] = jnp.concatenate(pieces(norm) + [blank], axis=0).astype(BF)

    @pl.when(side[0] == 0)
    def _():
        put(0, 1)

    @pl.when(side[0] != 0)
    def _():
        put(1, 0)


def merge_kernel(side, keep, got, keys, query, out, norm):
    for slot in range(2):
        rows = slice(slot * TOK, (slot + 1) * TOK)
        keys[slot * ROWS : slot * ROWS + TOK, :] = keep[rows, :]
        keys[slot * ROWS + TOK : (slot + 1) * ROWS, :] = got[rows, :]

    def put(first, second):
        for slot, dest in ((2, query), (3, out)):
            rows = slice(slot * TOK, (slot + 1) * TOK)
            dest[:TOK, :] = first[rows, :]
            dest[TOK:, :] = second[rows, :]
        norm[:AUX, :] = first[4 * TOK :, :]
        norm[AUX:, :] = second[4 * TOK :, :]

    @pl.when(side[0] == 0)
    def _():
        put(keep, got)

    @pl.when(side[0] != 0)
    def _():
        put(got, keep)


def delta_kernel(query, out, norm, dout, pay):
    pay[:ROWS, :] = query[...]
    pay[ROWS : 2 * ROWS, :] = dout[...]
    product = dout[...].astype(F32) * out[...].astype(F32)
    delta = jnp.sum(product.T, axis=0, keepdims=True)
    first = norm[:AUX, :].astype(F32)
    second = norm[AUX:, :].astype(F32)
    rows = (
        [first[:3, :], second[:3, :]]
        + pieces(delta[:, :TOK])
        + pieces(delta[:, TOK:])
        + [jnp.zeros((AUX - 12, TOK), F32)]
    )
    pay[2 * ROWS :, :] = jnp.concatenate(rows, axis=0).astype(BF)


def dot(left, right, left_dim, right_dim):
    return lax.dot_general(
        left, right, (((left_dim,), (right_dim,)), ((), ())), preferred_element_type=F32
    )


def row_of(aux, at):
    first = aux[at : at + 1, :] + aux[at + 1 : at + 2, :] + aux[at + 2 : at + 3, :]
    second = aux[at + 3 : at + 4, :] + aux[at + 4 : at + 5, :] + aux[at + 5 : at + 6, :]
    return jnp.concatenate([first, second], axis=1)


def pairs_kernel(
    pays, keys0, keys1, keys2, keys3, grads_q, own, send, keys, values, sum_k, sum_v
):
    for slot, shard in enumerate((keys0, keys1, keys2, keys3)):
        rows = slice(slot * ROWS, (slot + 1) * ROWS)
        keys[rows, :] = shard[:ROWS, :]
        values[rows, :] = shard[ROWS:, :]
    for block in range(GROUP):
        query = pays[block, :ROWS, :]
        dout = pays[block, ROWS : 2 * ROWS, :]
        aux = pays[block, 2 * ROWS :, :].astype(F32)
        norm, delta = row_of(aux, 0), row_of(aux, 6)
        grad_q = None
        for at in range(0, KEYS, CHUNK):
            rows = slice(at, at + CHUNK)
            key = keys[rows, :]
            probs = jnp.exp2(dot(key, query, 1, 1) * (FACTOR * LOG2E) - norm)
            dprobs = dot(values[rows, :], dout, 1, 1)
            dscore = (probs * (dprobs - delta)).astype(BF)
            part_v = dot(probs.astype(BF), dout, 1, 0)
            part_k = dot(dscore, query, 1, 0)
            part_q = dot(key, dscore, 0, 0)
            if block == 0:
                sum_k[rows, :] = part_k
                sum_v[rows, :] = part_v
            else:
                sum_k[rows, :] += part_k
                sum_v[rows, :] += part_v
            grad_q = part_q if at == 0 else grad_q + part_q
        grad_q = (grad_q * FACTOR).astype(BF)
        grads_q[block] = grad_q[:, :TOK]
        grads_q[GROUP + block] = grad_q[:, TOK:]
    for slot in range(GROUP):
        for half, dest in enumerate((own, send)):
            rows = slice(slot * ROWS + half * TOK, slot * ROWS + (half + 1) * TOK)
            dest[slot, :TOK, :] = (sum_k[rows, :] * FACTOR).astype(dest.dtype)
            dest[slot, TOK:, :] = sum_v[rows, :].astype(dest.dtype)


def fold_kernel(own, got, total, send1, send2, send3):
    for slot, dest in enumerate((total, send1, send2, send3)):
        dest[:, :HD] = own[slot].astype(dest.dtype)
        dest[:, HD:] = got[slot].astype(dest.dtype)


def join_kernel(side, parts_q, total, got1, got2, got3, grad_q, grad_k, grad_v):
    for head in range(2):
        sum_q = parts_q[head * GROUP].astype(F32)
        for at in range(1, GROUP):
            sum_q += parts_q[head * GROUP + at].astype(F32)
        grad_q[:, head * HD : (head + 1) * HD] = sum_q.T.astype(BF)
    sum_kv = total[...]
    for got in (got1, got2, got3):
        sum_kv += got[...].astype(F32)
    sum_kv = sum_kv.astype(BF)

    def put(first, second):
        for at, dest in enumerate((grad_k, grad_v)):
            rows = slice(at * TOK, (at + 1) * TOK)
            dest[:, :HD] = sum_kv[rows, first * HD : (first + 1) * HD]
            dest[:, HD:] = sum_kv[rows, second * HD : (second + 1) * HD]

    @pl.when(side[0] == 0)
    def _():
        put(0, 1)

    @pl.when(side[0] != 0)
    def _():
        put(1, 0)


def along(value, steps):
    pairs = []
    for at in range(RING):
        for core, shift in enumerate((steps, -steps)):
            pairs.append((2 * at + core, 2 * ((at + shift) % RING) + core))
    return lax.ppermute(value, ("z_hi", "z_lo", "core"), pairs)


def across(value):
    return lax.ppermute(value, "x_lo", [(0, 1), (1, 0)])


def body(query_rows, key_rows, value_rows, output_rows, grad_output, log_norm):
    side = lax.axis_index("x_lo").astype(jnp.int32).reshape(1)
    swap = ((4 * TOK + AUX, HD), BF)
    heads, keep, send = local(
        split_kernel,
        [((32, 8, HD), BF), swap, swap],
        side,
        *[
            pltpu.with_memory_space_constraint(rows, pltpu.HBM)
            for rows in (grad_output, key_rows, value_rows, query_rows, output_rows, log_norm.T)
        ],
        far=range(1, 7),
        scratch=(
            pltpu.VMEM((8, 32 * HD), BF),
            pltpu.VMEM((4, TOK, 2 * HD), BF),
            pltpu.VMEM((2, TOK), F32),
            pltpu.SemaphoreType.DMA,
            pltpu.SemaphoreType.DMA((4,)),
            pltpu.SemaphoreType.DMA,
        ),
    )
    dout = lax.all_to_all(heads, ("x_lo", "x_hi", "y", "core"), 0, 0, tiled=True)
    dout = dout.reshape(ROWS, HD)
    got = across(send)
    block = ((ROWS, HD), BF)
    pair = ((2 * ROWS, HD), BF)
    keys, query, out, norm = local(
        merge_kernel, [pair, block, block, ((2 * AUX, HD), BF)], side, keep, got
    )
    all_keys = [keys] + [along(keys, step) for step in K_STEPS]
    (pay,) = local(delta_kernel, [((PAY, HD), BF)], query, out, norm, dout)
    pays = lax.all_gather(pay, "z_hi")
    shards = ((GROUP, ROWS, HD), BF)
    parts_q, own, send = local(
        pairs_kernel,
        [((2 * GROUP, HD, TOK), BF), (shards[0], F32), shards],
        pays,
        *all_keys,
        scratch=(pltpu.VMEM((KEYS, HD), BF),) * 2 + (pltpu.VMEM((KEYS, HD), F32),) * 2,
    )
    got = across(send)
    parts_q = lax.all_to_all(parts_q, ("x_lo", "z_hi"), 0, 0, tiled=True)
    wide = ((ROWS, 2 * HD), BF)
    total, *sends = local(
        fold_kernel, [(wide[0], F32)] + [wide] * 3, own, got, cost=LONG
    )
    gots = [along(part, -step) for part, step in zip(sends, K_STEPS)]
    return tuple(
        local(join_kernel, [((TOK, 2 * HD), BF)] * 3, side, parts_q, total, *gots)
    )


def solution(mesh):
    fine = Mesh(
        mesh.devices.reshape(2, 4, 4, 2, 4, 2), ("x_lo", "z_hi", "z_lo", "x_hi", "y", "core")
    )
    blk, uly = ("x_lo", "z_hi", "z_lo"), ("x_hi", "y", "core")
    placed = P(blk, uly)
    return jax.shard_map(
        body,
        mesh=fine,
        in_specs=(placed, placed, placed, placed, P(blk + uly, None), placed),
        out_specs=(placed, placed, placed),
        check_vma=False,
    )
```

```python
import functools
import math

import jax
import jax.numpy as jnp
from jax import lax
from jax.experimental import pallas as pl
from jax.experimental.pallas import tpu as pltpu
from jax.sharding import Mesh, PartitionSpec as P

HD = 128
TOK = 128
ROWS = 2 * TOK
AUX = 16
PAY = 2 * ROWS + AUX
RING = 16
LOG2E = math.log2(math.e)
FACTOR = 1.0 / math.sqrt(HD)
BF = jnp.bfloat16
F32 = jnp.float32
KEYS = 4 * ROWS
CHUNK = 512
LONG = pl.CostEstimate(flops=10**11, bytes_accessed=10**8, transcendentals=0)
K_STEPS = (1, -1, -2)
GROUP = 4


def pieces(value):
    high = value.astype(BF)
    rest = value - high.astype(F32)
    mid = rest.astype(BF)
    low = (rest - mid.astype(F32)).astype(BF)
    return [high.astype(F32), mid.astype(F32), low.astype(F32)]


def local(kernel, outs, *args, far=(), scratch=(), cost=None):
    scalars = [pl.BlockSpec(memory_space=pltpu.SMEM)]
    whole = [pl.BlockSpec(memory_space=pltpu.VMEM)]
    return pl.pallas_call(
        kernel,
        out_shape=[jax.ShapeDtypeStruct(shape, dtype) for shape, dtype in outs],
        in_specs=[
            pl.BlockSpec(memory_space=pltpu.HBM)
            if at in far
            else (scalars if arg.dtype == jnp.int32 else whole)[0]
            for at, arg in enumerate(args)
        ],
        out_specs=whole * len(outs),
        scratch_shapes=list(scratch),
        cost_estimate=cost,
        compiler_params=pltpu.CompilerParams(vmem_limit_bytes=48 * 1024 * 1024),
    )(*args)


def split_kernel(side, key, value, query, out, lnorm, keep, send, norm_in, sems):
    copies = [pltpu.make_async_copy(lnorm, norm_in, sems.at[8])]
    for slot, rows in enumerate((key, value, query, out)):
        for to, (head, dest) in enumerate(((side[0], keep), (1 - side[0], send))):
            columns = pl.ds(pl.multiple_of(head * HD, HD), HD)
            target = dest.at[pl.ds(slot * TOK, TOK)]
            copies.append(
                pltpu.make_async_copy(rows.at[:, columns], target, sems.at[2 * slot + to])
            )
    for copy in copies:
        copy.start()
    copies[0].wait()

    def put(first, second):
        for head, dest in enumerate((first, second)):
            norm = norm_in[head : head + 1, :] * LOG2E
            blank = jnp.zeros((AUX - 3, TOK), F32)
            dest[4 * TOK :, :] = jnp.concatenate(pieces(norm) + [blank], axis=0).astype(BF)

    @pl.when(side[0] == 0)
    def _():
        put(keep, send)

    @pl.when(side[0] != 0)
    def _():
        put(send, keep)

    for copy in copies[1:]:
        copy.wait()


def merge_kernel(side, keep, got, keys, query, out, norm):
    for slot in range(2):
        rows = slice(slot * TOK, (slot + 1) * TOK)
        keys[slot * ROWS : slot * ROWS + TOK, :] = keep[rows, :]
        keys[slot * ROWS + TOK : (slot + 1) * ROWS, :] = got[rows, :]

    def put(first, second):
        for slot, dest in ((2, query), (3, out)):
            rows = slice(slot * TOK, (slot + 1) * TOK)
            dest[:TOK, :] = first[rows, :]
            dest[TOK:, :] = second[rows, :]
        norm[:AUX, :] = first[4 * TOK :, :]
        norm[AUX:, :] = second[4 * TOK :, :]

    @pl.when(side[0] == 0)
    def _():
        put(keep, got)

    @pl.when(side[0] != 0)
    def _():
        put(got, keep)


def delta_kernel(query, out, norm, dout, pay):
    pay[:ROWS, :] = query[...]
    blocks = dout[...].astype(F32).reshape(16, 2, 8, HD)
    ordered = jnp.concatenate([blocks[:, at].reshape(TOK, HD) for at in range(2)], axis=0)
    pay[ROWS : 2 * ROWS, :] = ordered.astype(BF)
    product = ordered * out[...].astype(F32)
    delta = jnp.sum(product.T, axis=0, keepdims=True)
    first = norm[:AUX, :].astype(F32)
    second = norm[AUX:, :].astype(F32)
    rows = (
        [first[:3, :], second[:3, :]]
        + pieces(delta[:, :TOK])
        + pieces(delta[:, TOK:])
        + [jnp.zeros((AUX - 12, TOK), F32)]
    )
    pay[2 * ROWS :, :] = jnp.concatenate(rows, axis=0).astype(BF)


def dot(left, right, left_dim, right_dim):
    return lax.dot_general(
        left, right, (((left_dim,), (right_dim,)), ((), ())), preferred_element_type=F32
    )


def row_of(aux, at):
    first = aux[at : at + 1, :] + aux[at + 1 : at + 2, :] + aux[at + 2 : at + 3, :]
    second = aux[at + 3 : at + 4, :] + aux[at + 4 : at + 5, :] + aux[at + 5 : at + 6, :]
    return jnp.concatenate([first, second], axis=1)


def pairs_kernel(
    pays, keys0, keys1, keys2, keys3, grads_q, own, send, keys, values, sum_k, sum_v
):
    for slot, shard in enumerate((keys0, keys1, keys2, keys3)):
        rows = slice(slot * ROWS, (slot + 1) * ROWS)
        keys[rows, :] = shard[:ROWS, :]
        values[rows, :] = shard[ROWS:, :]
    query = jnp.concatenate([pays[at, :ROWS, :] for at in range(GROUP)], axis=0)
    dout = jnp.concatenate([pays[at, ROWS : 2 * ROWS, :] for at in range(GROUP)], axis=0)
    aux = [pays[at, 2 * ROWS :, :].astype(F32) for at in range(GROUP)]
    norm = jnp.concatenate([row_of(rows, 0) for rows in aux], axis=1)
    delta = jnp.concatenate([row_of(rows, 6) for rows in aux], axis=1)
    grad_q = None
    for at in range(0, KEYS, CHUNK):
        rows = slice(at, at + CHUNK)
        key = keys[rows, :]
        probs = jnp.exp2(dot(key, query, 1, 1) * (FACTOR * LOG2E) - norm)
        dprobs = dot(values[rows, :], dout, 1, 1)
        dscore = (probs * (dprobs - delta)).astype(BF)
        sum_v[rows, :] = dot(probs.astype(BF), dout, 1, 0)
        sum_k[rows, :] = dot(dscore, query, 1, 0)
        part_q = dot(key, dscore, 0, 0)
        grad_q = part_q if at == 0 else grad_q + part_q
    grad_q = (grad_q * FACTOR).astype(BF)
    for at in range(GROUP):
        grads_q[at] = grad_q[:, at * ROWS : at * ROWS + TOK]
        grads_q[GROUP + at] = grad_q[:, at * ROWS + TOK : (at + 1) * ROWS]
    for slot in range(GROUP):
        for half, dest in enumerate((own, send)):
            rows = slice(slot * ROWS + half * TOK, slot * ROWS + (half + 1) * TOK)
            dest[slot, :TOK, :] = (sum_k[rows, :] * FACTOR).astype(dest.dtype)
            dest[slot, TOK:, :] = sum_v[rows, :].astype(dest.dtype)


def fold_kernel(own, got, total, send1, send2, send3):
    for slot, dest in enumerate((total, send1, send2, send3)):
        dest[:, :HD] = own[slot].astype(dest.dtype)
        dest[:, HD:] = got[slot].astype(dest.dtype)


def join_kernel(side, parts_q, total, got1, got2, got3, grad_q, grad_k, grad_v):
    for head in range(2):
        sum_q = parts_q[head * GROUP].astype(F32)
        for at in range(1, GROUP):
            sum_q += parts_q[head * GROUP + at].astype(F32)
        grad_q[:, head * HD : (head + 1) * HD] = sum_q.T.astype(BF)
    sum_kv = total[...]
    for got in (got1, got2, got3):
        sum_kv += got[...].astype(F32)
    sum_kv = sum_kv.astype(BF)

    def put(first, second):
        for at, dest in enumerate((grad_k, grad_v)):
            rows = slice(at * TOK, (at + 1) * TOK)
            dest[:, :HD] = sum_kv[rows, first * HD : (first + 1) * HD]
            dest[:, HD:] = sum_kv[rows, second * HD : (second + 1) * HD]

    @pl.when(side[0] == 0)
    def _():
        put(0, 1)

    @pl.when(side[0] != 0)
    def _():
        put(1, 0)


def along(value, steps):
    pairs = []
    for at in range(RING):
        for core, shift in enumerate((steps, -steps)):
            pairs.append((2 * at + core, 2 * ((at + shift) % RING) + core))
    return lax.ppermute(value, ("z_hi", "z_lo", "core"), pairs)


def across(value):
    return lax.ppermute(value, "x_lo", [(0, 1), (1, 0)])


def body(query_rows, key_rows, value_rows, output_rows, grad_output, log_norm):
    side = lax.axis_index("x_lo").astype(jnp.int32).reshape(1)
    swap = ((4 * TOK + AUX, HD), BF)
    dout = lax.all_to_all(grad_output, ("x_hi", "y", "core", "x_lo"), 1, 0, tiled=True)
    keep, send = local(
        split_kernel,
        [swap, swap],
        side,
        *[
            pltpu.with_memory_space_constraint(rows, pltpu.HBM)
            for rows in (key_rows, value_rows, query_rows, output_rows, log_norm.T)
        ],
        far=range(1, 6),
        scratch=(pltpu.VMEM((2, TOK), F32), pltpu.SemaphoreType.DMA((9,))),
    )
    got = across(send)
    block = ((ROWS, HD), BF)
    pair = ((2 * ROWS, HD), BF)
    keys, query, out, norm = local(
        merge_kernel, [pair, block, block, ((2 * AUX, HD), BF)], side, keep, got
    )
    all_keys = [keys] + [along(keys, step) for step in K_STEPS]
    (pay,) = local(delta_kernel, [((PAY, HD), BF)], query, out, norm, dout)
    pays = lax.all_gather(pay, "z_hi")
    shards = ((GROUP, ROWS, HD), BF)
    parts_q, own, send = local(
        pairs_kernel,
        [((2 * GROUP, HD, TOK), BF), (shards[0], F32), shards],
        pays,
        *all_keys,
        scratch=(pltpu.VMEM((KEYS, HD), BF),) * 2 + (pltpu.VMEM((KEYS, HD), F32),) * 2,
    )
    got = across(send)
    parts_q = lax.all_to_all(parts_q, ("x_lo", "z_hi"), 0, 0, tiled=True)
    wide = ((ROWS, 2 * HD), BF)
    total, *sends = local(
        fold_kernel, [(wide[0], F32)] + [wide] * 3, own, got, cost=LONG
    )
    gots = [along(part, -step) for part, step in zip(sends, K_STEPS)]
    return tuple(
        local(join_kernel, [((TOK, 2 * HD), BF)] * 3, side, parts_q, total, *gots)
    )


def solution(mesh):
    fine = Mesh(
        mesh.devices.reshape(2, 4, 4, 2, 4, 2), ("x_lo", "z_hi", "z_lo", "x_hi", "y", "core")
    )
    blk, uly = ("x_lo", "z_hi", "z_lo"), ("x_hi", "y", "core")
    placed = P(blk, uly)
    return jax.shard_map(
        body,
        mesh=fine,
        in_specs=(placed, placed, placed, placed, P(blk + uly, None), placed),
        out_specs=(placed, placed, placed),
        check_vma=False,
    )
```

```python
import functools
import math

import jax
import jax.numpy as jnp
from jax import lax
from jax.experimental import pallas as pl
from jax.experimental.pallas import tpu as pltpu
from jax.sharding import Mesh, PartitionSpec as P

HD = 128
TOK = 128
ROWS = 2 * TOK
AUX = 16
PAY = 2 * ROWS + AUX
RING = 16
LOG2E = math.log2(math.e)
FACTOR = 1.0 / math.sqrt(HD)
BF = jnp.bfloat16
F32 = jnp.float32
KEYS = 4 * ROWS
CHUNK = 512
LONG = pl.CostEstimate(flops=10**11, bytes_accessed=10**8, transcendentals=0)
K_STEPS = (1, -1, -2)
GROUP = 4


def pieces(value):
    high = value.astype(BF)
    rest = value - high.astype(F32)
    mid = rest.astype(BF)
    low = (rest - mid.astype(F32)).astype(BF)
    return [high.astype(F32), mid.astype(F32), low.astype(F32)]


def local(kernel, outs, *args, far=(), scratch=(), cost=None):
    scalars = [pl.BlockSpec(memory_space=pltpu.SMEM)]
    whole = [pl.BlockSpec(memory_space=pltpu.VMEM)]
    return pl.pallas_call(
        kernel,
        out_shape=[jax.ShapeDtypeStruct(shape, dtype) for shape, dtype in outs],
        in_specs=[
            pl.BlockSpec(memory_space=pltpu.HBM)
            if at in far
            else (scalars if arg.dtype == jnp.int32 else whole)[0]
            for at, arg in enumerate(args)
        ],
        out_specs=whole * len(outs),
        scratch_shapes=list(scratch),
        cost_estimate=cost,
        compiler_params=pltpu.CompilerParams(vmem_limit_bytes=48 * 1024 * 1024),
    )(*args)


def split_kernel(side, key, value, query, out, lnorm, keep, send, norm_in, sems):
    copies = [pltpu.make_async_copy(lnorm, norm_in, sems.at[8])]
    for slot, rows in enumerate((key, value, query, out)):
        for to, (head, dest) in enumerate(((side[0], keep), (1 - side[0], send))):
            columns = pl.ds(pl.multiple_of(head * HD, HD), HD)
            target = dest.at[pl.ds(slot * TOK, TOK)]
            copies.append(
                pltpu.make_async_copy(rows.at[:, columns], target, sems.at[2 * slot + to])
            )
    for copy in copies:
        copy.start()
    copies[0].wait()

    def put(first, second):
        for head, dest in enumerate((first, second)):
            norm = norm_in[head : head + 1, :] * LOG2E
            blank = jnp.zeros((AUX - 3, TOK), F32)
            dest[4 * TOK :, :] = jnp.concatenate(pieces(norm) + [blank], axis=0).astype(BF)

    @pl.when(side[0] == 0)
    def _():
        put(keep, send)

    @pl.when(side[0] != 0)
    def _():
        put(send, keep)

    for copy in copies[1:]:
        copy.wait()


def merge_kernel(side, keep, got, keys, query, out, norm):
    for slot in range(2):
        rows = slice(slot * TOK, (slot + 1) * TOK)
        keys[slot * ROWS : slot * ROWS + TOK, :] = keep[rows, :]
        keys[slot * ROWS + TOK : (slot + 1) * ROWS, :] = got[rows, :]

    def put(first, second):
        for slot, dest in ((2, query), (3, out)):
            rows = slice(slot * TOK, (slot + 1) * TOK)
            dest[:TOK, :] = first[rows, :]
            dest[TOK:, :] = second[rows, :]
        norm[:AUX, :] = first[4 * TOK :, :]
        norm[AUX:, :] = second[4 * TOK :, :]

    @pl.when(side[0] == 0)
    def _():
        put(keep, got)

    @pl.when(side[0] != 0)
    def _():
        put(got, keep)


def delta_kernel(query, out, norm, dout, pay):
    pay[:ROWS, :] = query[...]
    blocks = dout[...].astype(F32).reshape(16, 2, 8, HD)
    ordered = jnp.concatenate([blocks[:, at].reshape(TOK, HD) for at in range(2)], axis=0)
    pay[ROWS : 2 * ROWS, :] = ordered.astype(BF)
    product = ordered * out[...].astype(F32)
    delta = jnp.sum(product.T, axis=0, keepdims=True)
    first = norm[:AUX, :].astype(F32)
    second = norm[AUX:, :].astype(F32)
    rows = (
        [first[:3, :], second[:3, :]]
        + pieces(delta[:, :TOK])
        + pieces(delta[:, TOK:])
        + [jnp.zeros((AUX - 12, TOK), F32)]
    )
    pay[2 * ROWS :, :] = jnp.concatenate(rows, axis=0).astype(BF)


def dot(left, right, left_dim, right_dim):
    return lax.dot_general(
        left, right, (((left_dim,), (right_dim,)), ((), ())), preferred_element_type=F32
    )


def row_of(aux, at):
    first = aux[at : at + 1, :] + aux[at + 1 : at + 2, :] + aux[at + 2 : at + 3, :]
    second = aux[at + 3 : at + 4, :] + aux[at + 4 : at + 5, :] + aux[at + 5 : at + 6, :]
    return jnp.concatenate([first, second], axis=1)


def pairs_kernel(
    pays, keys0, keys1, keys2, keys3, grads_q, own, send, keys, values, sum_k, sum_v
):
    for slot, shard in enumerate((keys0, keys1, keys2, keys3)):
        rows = slice(slot * ROWS, (slot + 1) * ROWS)
        keys[rows, :] = shard[:ROWS, :]
        values[rows, :] = shard[ROWS:, :]
    query = jnp.concatenate([pays[at, :ROWS, :] for at in range(GROUP)], axis=0)
    dout = jnp.concatenate([pays[at, ROWS : 2 * ROWS, :] for at in range(GROUP)], axis=0)
    aux = [pays[at, 2 * ROWS :, :].astype(F32) for at in range(GROUP)]
    norm = jnp.concatenate([row_of(rows, 0) for rows in aux], axis=1)
    delta = jnp.concatenate([row_of(rows, 6) for rows in aux], axis=1)
    grad_q = None
    for at in range(0, KEYS, CHUNK):
        rows = slice(at, at + CHUNK)
        key = keys[rows, :]
        probs = jnp.exp2(dot(key, query, 1, 1) * (FACTOR * LOG2E) - norm)
        dprobs = dot(values[rows, :], dout, 1, 1)
        dscore = (probs * (dprobs - delta)).astype(BF)
        sum_v[rows, :] = dot(probs.astype(BF), dout, 1, 0)
        sum_k[rows, :] = dot(dscore, query, 1, 0)
        part_q = dot(key, dscore, 0, 0)
        grad_q = part_q if at == 0 else grad_q + part_q
    grad_q = (grad_q * FACTOR).astype(BF)
    for at in range(GROUP):
        grads_q[at] = grad_q[:, at * ROWS : at * ROWS + TOK]
        grads_q[GROUP + at] = grad_q[:, at * ROWS + TOK : (at + 1) * ROWS]
    for slot in range(GROUP):
        for half, dest in enumerate((own, send)):
            rows = slice(slot * ROWS + half * TOK, slot * ROWS + (half + 1) * TOK)
            dest[slot, :TOK, :] = (sum_k[rows, :] * FACTOR).astype(dest.dtype)
            dest[slot, TOK:, :] = sum_v[rows, :].astype(dest.dtype)


def fold_kernel(own, got, total, send1, send2, send3):
    for slot, dest in enumerate((total, send1, send2, send3)):
        dest[:, :HD] = own[slot].astype(dest.dtype)
        dest[:, HD:] = got[slot].astype(dest.dtype)


def query_kernel(parts_q, grad_q):
    for head in range(2):
        sum_q = parts_q[head * GROUP].astype(F32)
        for at in range(1, GROUP):
            sum_q += parts_q[head * GROUP + at].astype(F32)
        grad_q[:, head * HD : (head + 1) * HD] = sum_q.T.astype(BF)


def join_kernel(side, total, got1, got2, got3, grad_k, grad_v):
    sum_kv = total[...]
    for got in (got1, got2, got3):
        sum_kv += got[...].astype(F32)
    sum_kv = sum_kv.astype(BF)

    def put(first, second):
        for at, dest in enumerate((grad_k, grad_v)):
            rows = slice(at * TOK, (at + 1) * TOK)
            dest[:, :HD] = sum_kv[rows, first * HD : (first + 1) * HD]
            dest[:, HD:] = sum_kv[rows, second * HD : (second + 1) * HD]

    @pl.when(side[0] == 0)
    def _():
        put(0, 1)

    @pl.when(side[0] != 0)
    def _():
        put(1, 0)


def along(value, steps):
    pairs = []
    for at in range(RING):
        for core, shift in enumerate((steps, -steps)):
            pairs.append((2 * at + core, 2 * ((at + shift) % RING) + core))
    return lax.ppermute(value, ("z_hi", "z_lo", "core"), pairs)


def across(value):
    return lax.ppermute(value, "x_lo", [(0, 1), (1, 0)])


def body(query_rows, key_rows, value_rows, output_rows, grad_output, log_norm):
    side = lax.axis_index("x_lo").astype(jnp.int32).reshape(1)
    swap = ((4 * TOK + AUX, HD), BF)
    dout = lax.all_to_all(grad_output, ("x_hi", "y", "core", "x_lo"), 1, 0, tiled=True)
    keep, send = local(
        split_kernel,
        [swap, swap],
        side,
        *[
            pltpu.with_memory_space_constraint(rows, pltpu.HBM)
            for rows in (key_rows, value_rows, query_rows, output_rows, log_norm.T)
        ],
        far=range(1, 6),
        scratch=(pltpu.VMEM((2, TOK), F32), pltpu.SemaphoreType.DMA((9,))),
    )
    got = across(send)
    block = ((ROWS, HD), BF)
    pair = ((2 * ROWS, HD), BF)
    keys, query, out, norm = local(
        merge_kernel, [pair, block, block, ((2 * AUX, HD), BF)], side, keep, got
    )
    all_keys = [keys] + [along(keys, step) for step in K_STEPS]
    (pay,) = local(delta_kernel, [((PAY, HD), BF)], query, out, norm, dout)
    pays = lax.all_gather(pay, "z_hi")
    shards = ((GROUP, ROWS, HD), BF)
    parts_q, own, send = local(
        pairs_kernel,
        [((2 * GROUP, HD, TOK), BF), (shards[0], F32), shards],
        pays,
        *all_keys,
        scratch=(pltpu.VMEM((KEYS, HD), BF),) * 2 + (pltpu.VMEM((KEYS, HD), F32),) * 2,
    )
    got = across(send)
    parts_q = lax.all_to_all(parts_q, ("x_lo", "z_hi"), 0, 0, tiled=True)
    wide = ((ROWS, 2 * HD), BF)
    total, *sends = local(
        fold_kernel, [(wide[0], F32)] + [wide] * 3, own, got, cost=LONG
    )
    gots = [along(part, -step) for part, step in zip(sends, K_STEPS)]
    final = ((TOK, 2 * HD), BF)
    (grad_q,) = local(query_kernel, [final], parts_q)
    grad_q, gots[0] = lax.optimization_barrier((grad_q, gots[0]))
    grad_k, grad_v = local(join_kernel, [final] * 2, side, total, *gots)
    return grad_q, grad_k, grad_v


def solution(mesh):
    fine = Mesh(
        mesh.devices.reshape(2, 4, 4, 2, 4, 2), ("x_lo", "z_hi", "z_lo", "x_hi", "y", "core")
    )
    blk, uly = ("x_lo", "z_hi", "z_lo"), ("x_hi", "y", "core")
    placed = P(blk, uly)
    return jax.shard_map(
        body,
        mesh=fine,
        in_specs=(placed, placed, placed, placed, P(blk + uly, None), placed),
        out_specs=(placed, placed, placed),
        check_vma=False,
    )
```

```python
import functools
import math

import jax
import jax.numpy as jnp
from jax import lax
from jax.experimental import pallas as pl
from jax.experimental.pallas import tpu as pltpu
from jax.sharding import Mesh, PartitionSpec as P

HD = 128
TOK = 128
ROWS = 2 * TOK
AUX = 16
PAY = 2 * ROWS + AUX
RING = 16
LOG2E = math.log2(math.e)
FACTOR = 1.0 / math.sqrt(HD)
BF = jnp.bfloat16
F32 = jnp.float32
KEYS = 4 * ROWS
CHUNK = 512
LONG = pl.CostEstimate(flops=10**11, bytes_accessed=10**8, transcendentals=0)
K_STEPS = (1, -1, -2)
GROUP = 4


def pieces(value):
    high = value.astype(BF)
    rest = value - high.astype(F32)
    mid = rest.astype(BF)
    low = (rest - mid.astype(F32)).astype(BF)
    return [high.astype(F32), mid.astype(F32), low.astype(F32)]


def local(kernel, outs, *args, far=(), near=(), scratch=(), cost=None):
    scalars = [pl.BlockSpec(memory_space=pltpu.SMEM)]
    whole = [pl.BlockSpec(memory_space=pltpu.VMEM)]
    return pl.pallas_call(
        kernel,
        out_shape=[
            (pltpu.VMEM if at in near else jax.ShapeDtypeStruct)(shape, dtype)
            for at, (shape, dtype) in enumerate(outs)
        ],
        in_specs=[
            pl.BlockSpec(memory_space=pltpu.HBM)
            if at in far
            else (scalars if arg.dtype == jnp.int32 else whole)[0]
            for at, arg in enumerate(args)
        ],
        out_specs=whole * len(outs),
        scratch_shapes=list(scratch),
        cost_estimate=cost,
        compiler_params=pltpu.CompilerParams(vmem_limit_bytes=48 * 1024 * 1024),
    )(*args)


def split_kernel(side, key, value, query, out, lnorm, keep, send, norm_in, sems):
    copies = [pltpu.make_async_copy(lnorm, norm_in, sems.at[8])]
    for slot, rows in enumerate((key, value, query, out)):
        for to, (head, dest) in enumerate(((side[0], keep), (1 - side[0], send))):
            columns = pl.ds(pl.multiple_of(head * HD, HD), HD)
            target = dest.at[pl.ds(slot * TOK, TOK)]
            copies.append(
                pltpu.make_async_copy(rows.at[:, columns], target, sems.at[2 * slot + to])
            )
    for copy in copies:
        copy.start()
    copies[0].wait()

    def put(first, second):
        for head, dest in enumerate((first, second)):
            norm = norm_in[head : head + 1, :] * LOG2E
            blank = jnp.zeros((AUX - 3, TOK), F32)
            dest[4 * TOK :, :] = jnp.concatenate(pieces(norm) + [blank], axis=0).astype(BF)

    @pl.when(side[0] == 0)
    def _():
        put(keep, send)

    @pl.when(side[0] != 0)
    def _():
        put(send, keep)

    for copy in copies[1:]:
        copy.wait()


def merge_kernel(side, keep, got, keys, query, out, norm):
    for slot in range(2):
        rows = slice(slot * TOK, (slot + 1) * TOK)
        keys[slot * ROWS : slot * ROWS + TOK, :] = keep[rows, :]
        keys[slot * ROWS + TOK : (slot + 1) * ROWS, :] = got[rows, :]

    def put(first, second):
        for slot, dest in ((2, query), (3, out)):
            rows = slice(slot * TOK, (slot + 1) * TOK)
            dest[:TOK, :] = first[rows, :]
            dest[TOK:, :] = second[rows, :]
        norm[:AUX, :] = first[4 * TOK :, :]
        norm[AUX:, :] = second[4 * TOK :, :]

    @pl.when(side[0] == 0)
    def _():
        put(keep, got)

    @pl.when(side[0] != 0)
    def _():
        put(got, keep)


def delta_kernel(query, out, norm, dout, pay):
    pay[:ROWS, :] = query[...]
    blocks = dout[...].astype(F32).reshape(16, 2, 8, HD)
    ordered = jnp.concatenate([blocks[:, at].reshape(TOK, HD) for at in range(2)], axis=0)
    pay[ROWS : 2 * ROWS, :] = ordered.astype(BF)
    product = ordered * out[...].astype(F32)
    delta = jnp.sum(product.T, axis=0, keepdims=True)
    first = norm[:AUX, :].astype(F32)
    second = norm[AUX:, :].astype(F32)
    rows = (
        [first[:3, :], second[:3, :]]
        + pieces(delta[:, :TOK])
        + pieces(delta[:, TOK:])
        + [jnp.zeros((AUX - 12, TOK), F32)]
    )
    pay[2 * ROWS :, :] = jnp.concatenate(rows, axis=0).astype(BF)


def dot(left, right, left_dim, right_dim):
    return lax.dot_general(
        left, right, (((left_dim,), (right_dim,)), ((), ())), preferred_element_type=F32
    )


def row_of(aux, at):
    first = aux[at : at + 1, :] + aux[at + 1 : at + 2, :] + aux[at + 2 : at + 3, :]
    second = aux[at + 3 : at + 4, :] + aux[at + 4 : at + 5, :] + aux[at + 5 : at + 6, :]
    return jnp.concatenate([first, second], axis=1)


def pairs_kernel(
    pays, keys0, keys1, keys2, keys3, grads_q, own, send, keys, values, sum_k, sum_v
):
    for slot, shard in enumerate((keys0, keys1, keys2, keys3)):
        rows = slice(slot * ROWS, (slot + 1) * ROWS)
        keys[rows, :] = shard[:ROWS, :]
        values[rows, :] = shard[ROWS:, :]
    query = jnp.concatenate([pays[at, :ROWS, :] for at in range(GROUP)], axis=0)
    dout = jnp.concatenate([pays[at, ROWS : 2 * ROWS, :] for at in range(GROUP)], axis=0)
    aux = [pays[at, 2 * ROWS :, :].astype(F32) for at in range(GROUP)]
    norm = jnp.concatenate([row_of(rows, 0) for rows in aux], axis=1)
    delta = jnp.concatenate([row_of(rows, 6) for rows in aux], axis=1)
    grad_q = None
    for at in range(0, KEYS, CHUNK):
        rows = slice(at, at + CHUNK)
        key = keys[rows, :]
        probs = jnp.exp2(dot(key, query, 1, 1) * (FACTOR * LOG2E) - norm)
        dprobs = dot(values[rows, :], dout, 1, 1)
        dscore = (probs * (dprobs - delta)).astype(BF)
        sum_v[rows, :] = dot(probs.astype(BF), dout, 1, 0)
        sum_k[rows, :] = dot(dscore, query, 1, 0)
        part_q = dot(key, dscore, 0, 0)
        grad_q = part_q if at == 0 else grad_q + part_q
    grad_q = (grad_q * FACTOR).astype(BF)
    for at in range(GROUP):
        grads_q[at] = grad_q[:, at * ROWS : at * ROWS + TOK]
        grads_q[GROUP + at] = grad_q[:, at * ROWS + TOK : (at + 1) * ROWS]
    for slot in range(GROUP):
        for half, dest in enumerate((own, send)):
            rows = slice(slot * ROWS + half * TOK, slot * ROWS + (half + 1) * TOK)
            dest[slot, :TOK, :] = (sum_k[rows, :] * FACTOR).astype(dest.dtype)
            dest[slot, TOK:, :] = sum_v[rows, :].astype(dest.dtype)


def fold_kernel(own, got, total, send1, send2, send3):
    for slot, dest in enumerate((total, send1, send2, send3)):
        dest[:, :HD] = own[slot].astype(dest.dtype)
        dest[:, HD:] = got[slot].astype(dest.dtype)


def join_kernel(side, parts_q, total, got1, got2, got3, grad_q, grad_k, grad_v):
    for head in range(2):
        sum_q = parts_q[head * GROUP].astype(F32)
        for at in range(1, GROUP):
            sum_q += parts_q[head * GROUP + at].astype(F32)
        grad_q[:, head * HD : (head + 1) * HD] = sum_q.T.astype(BF)
    sum_kv = total[...]
    for got in (got1, got2, got3):
        sum_kv += got[...].astype(F32)
    sum_kv = sum_kv.astype(BF)

    def put(first, second):
        for at, dest in enumerate((grad_k, grad_v)):
            rows = slice(at * TOK, (at + 1) * TOK)
            dest[:, :HD] = sum_kv[rows, first * HD : (first + 1) * HD]
            dest[:, HD:] = sum_kv[rows, second * HD : (second + 1) * HD]

    @pl.when(side[0] == 0)
    def _():
        put(0, 1)

    @pl.when(side[0] != 0)
    def _():
        put(1, 0)


def along(value, steps):
    pairs = []
    for at in range(RING):
        for core, shift in enumerate((steps, -steps)):
            pairs.append((2 * at + core, 2 * ((at + shift) % RING) + core))
    return lax.ppermute(value, ("z_hi", "z_lo", "core"), pairs)


def across(value):
    return lax.ppermute(value, "x_lo", [(0, 1), (1, 0)])


def body(query_rows, key_rows, value_rows, output_rows, grad_output, log_norm):
    side = lax.axis_index("x_lo").astype(jnp.int32).reshape(1)
    swap = ((4 * TOK + AUX, HD), BF)
    dout = lax.all_to_all(grad_output, ("x_hi", "y", "core", "x_lo"), 1, 0, tiled=True)
    keep, send = local(
        split_kernel,
        [swap, swap],
        side,
        *[
            pltpu.with_memory_space_constraint(rows, pltpu.HBM)
            for rows in (key_rows, value_rows, query_rows, output_rows, log_norm.T)
        ],
        far=range(1, 6),
        scratch=(pltpu.VMEM((2, TOK), F32), pltpu.SemaphoreType.DMA((9,))),
    )
    got = across(send)
    block = ((ROWS, HD), BF)
    pair = ((2 * ROWS, HD), BF)
    keys, query, out, norm = local(
        merge_kernel, [pair, block, block, ((2 * AUX, HD), BF)], side, keep, got
    )
    all_keys = [keys] + [along(keys, step) for step in K_STEPS]
    (pay,) = local(delta_kernel, [((PAY, HD), BF)], query, out, norm, dout)
    pays = lax.all_gather(pay, "z_hi")
    shards = ((GROUP, ROWS, HD), BF)
    parts_q, own, send = local(
        pairs_kernel,
        [((2 * GROUP, HD, TOK), BF), (shards[0], F32), shards],
        pays,
        *all_keys,
        near=(0,),
        scratch=(pltpu.VMEM((KEYS, HD), BF),) * 2 + (pltpu.VMEM((KEYS, HD), F32),) * 2,
    )
    got = across(send)
    parts_q = lax.all_to_all(parts_q, ("x_lo", "z_hi"), 0, 0, tiled=True)
    wide = ((ROWS, 2 * HD), BF)
    total, *sends = local(
        fold_kernel, [(wide[0], F32)] + [wide] * 3, own, got, cost=LONG
    )
    gots = [along(part, -step) for part, step in zip(sends, K_STEPS)]
    return tuple(
        local(join_kernel, [((TOK, 2 * HD), BF)] * 3, side, parts_q, total, *gots)
    )


def solution(mesh):
    fine = Mesh(
        mesh.devices.reshape(2, 4, 4, 2, 4, 2), ("x_lo", "z_hi", "z_lo", "x_hi", "y", "core")
    )
    blk, uly = ("x_lo", "z_hi", "z_lo"), ("x_hi", "y", "core")
    placed = P(blk, uly)
    return jax.shard_map(
        body,
        mesh=fine,
        in_specs=(placed, placed, placed, placed, P(blk + uly, None), placed),
        out_specs=(placed, placed, placed),
        check_vma=False,
    )
```

```python
import functools
import math

import jax
import jax.numpy as jnp
from jax import lax
from jax.experimental import pallas as pl
from jax.experimental.pallas import tpu as pltpu
from jax.sharding import Mesh, PartitionSpec as P

HD = 128
TOK = 128
ROWS = 2 * TOK
AUX = 16
PAY = 2 * ROWS + AUX
RING = 16
LOG2E = math.log2(math.e)
FACTOR = 1.0 / math.sqrt(HD)
BF = jnp.bfloat16
F32 = jnp.float32
KEYS = 4 * ROWS
CHUNK = 512
LONG = pl.CostEstimate(flops=10**11, bytes_accessed=10**8, transcendentals=0)
K_STEPS = (1, -1, -2)
GROUP = 4


def pieces(value):
    high = value.astype(BF)
    rest = value - high.astype(F32)
    mid = rest.astype(BF)
    low = (rest - mid.astype(F32)).astype(BF)
    return [high.astype(F32), mid.astype(F32), low.astype(F32)]


def local(kernel, outs, *args, far=(), scratch=(), cost=None):
    scalars = [pl.BlockSpec(memory_space=pltpu.SMEM)]
    whole = [pl.BlockSpec(memory_space=pltpu.VMEM)]
    return pl.pallas_call(
        kernel,
        out_shape=[jax.ShapeDtypeStruct(shape, dtype) for shape, dtype in outs],
        in_specs=[
            pl.BlockSpec(memory_space=pltpu.HBM)
            if at in far
            else (scalars if arg.dtype == jnp.int32 else whole)[0]
            for at, arg in enumerate(args)
        ],
        out_specs=whole * len(outs),
        scratch_shapes=list(scratch),
        cost_estimate=cost,
        compiler_params=pltpu.CompilerParams(vmem_limit_bytes=48 * 1024 * 1024),
    )(*args)


def split_kernel(side, key, value, query, out, lnorm, keep, send, norm_in, sems):
    copies = [pltpu.make_async_copy(lnorm, norm_in, sems.at[8])]
    for slot, rows in enumerate((key, value, query, out)):
        for to, (head, dest) in enumerate(((side[0], keep), (1 - side[0], send))):
            columns = pl.ds(pl.multiple_of(head * HD, HD), HD)
            target = dest.at[pl.ds(slot * TOK, TOK)]
            copies.append(
                pltpu.make_async_copy(rows.at[:, columns], target, sems.at[2 * slot + to])
            )
    for copy in copies:
        copy.start()
    copies[0].wait()

    def put(first, second):
        for head, dest in enumerate((first, second)):
            norm = norm_in[head : head + 1, :] * LOG2E
            blank = jnp.zeros((AUX - 3, TOK), F32)
            dest[4 * TOK :, :] = jnp.concatenate(pieces(norm) + [blank], axis=0).astype(BF)

    @pl.when(side[0] == 0)
    def _():
        put(keep, send)

    @pl.when(side[0] != 0)
    def _():
        put(send, keep)

    for copy in copies[1:]:
        copy.wait()


def merge_kernel(keep, got, keys):
    for slot in range(2):
        rows = slice(slot * TOK, (slot + 1) * TOK)
        keys[slot * ROWS : slot * ROWS + TOK, :] = keep[rows, :]
        keys[slot * ROWS + TOK : (slot + 1) * ROWS, :] = got[rows, :]


def delta_kernel(side, keep, got, dout, pay):
    blocks = dout[...].astype(F32).reshape(16, 2, 8, HD)

    def put(sources):
        norms, deltas = [], []
        for half, source in enumerate(sources):
            rows = slice(half * TOK, (half + 1) * TOK)
            ordered = blocks[:, half].reshape(TOK, HD)
            pay[rows, :] = source[2 * TOK : 3 * TOK, :]
            pay[ROWS + half * TOK : ROWS + (half + 1) * TOK, :] = ordered.astype(BF)
            product = ordered * source[3 * TOK : 4 * TOK, :].astype(F32)
            deltas += pieces(jnp.sum(product.T, axis=0, keepdims=True))
            norms.append(source[4 * TOK :, :].astype(F32)[:3, :])
        rows = norms + deltas + [jnp.zeros((AUX - 12, TOK), F32)]
        pay[2 * ROWS :, :] = jnp.concatenate(rows, axis=0).astype(BF)

    @pl.when(side[0] == 0)
    def _():
        put((keep, got))

    @pl.when(side[0] != 0)
    def _():
        put((got, keep))


def dot(left, right, left_dim, right_dim):
    return lax.dot_general(
        left, right, (((left_dim,), (right_dim,)), ((), ())), preferred_element_type=F32
    )


def row_of(aux, at):
    first = aux[at : at + 1, :] + aux[at + 1 : at + 2, :] + aux[at + 2 : at + 3, :]
    second = aux[at + 3 : at + 4, :] + aux[at + 4 : at + 5, :] + aux[at + 5 : at + 6, :]
    return jnp.concatenate([first, second], axis=1)


def pairs_kernel(
    pays, keys0, keys1, keys2, keys3, grads_q, own, send, keys, values, sum_k, sum_v
):
    for slot, shard in enumerate((keys0, keys1, keys2, keys3)):
        rows = slice(slot * ROWS, (slot + 1) * ROWS)
        keys[rows, :] = shard[:ROWS, :]
        values[rows, :] = shard[ROWS:, :]
    query = jnp.concatenate([pays[at, :ROWS, :] for at in range(GROUP)], axis=0)
    dout = jnp.concatenate([pays[at, ROWS : 2 * ROWS, :] for at in range(GROUP)], axis=0)
    aux = [pays[at, 2 * ROWS :, :].astype(F32) for at in range(GROUP)]
    norm = jnp.concatenate([row_of(rows, 0) for rows in aux], axis=1)
    delta = jnp.concatenate([row_of(rows, 6) for rows in aux], axis=1)
    grad_q = None
    for at in range(0, KEYS, CHUNK):
        rows = slice(at, at + CHUNK)
        key = keys[rows, :]
        probs = jnp.exp2(dot(key, query, 1, 1) * (FACTOR * LOG2E) - norm)
        dprobs = dot(values[rows, :], dout, 1, 1)
        dscore = (probs * (dprobs - delta)).astype(BF)
        sum_v[rows, :] = dot(probs.astype(BF), dout, 1, 0)
        sum_k[rows, :] = dot(dscore, query, 1, 0)
        part_q = dot(key, dscore, 0, 0)
        grad_q = part_q if at == 0 else grad_q + part_q
    grad_q = (grad_q * FACTOR).astype(BF)
    for at in range(GROUP):
        grads_q[at] = grad_q[:, at * ROWS : at * ROWS + TOK]
        grads_q[GROUP + at] = grad_q[:, at * ROWS + TOK : (at + 1) * ROWS]
    for slot in range(GROUP):
        for half, dest in enumerate((own, send)):
            rows = slice(slot * ROWS + half * TOK, slot * ROWS + (half + 1) * TOK)
            dest[slot, :TOK, :] = (sum_k[rows, :] * FACTOR).astype(dest.dtype)
            dest[slot, TOK:, :] = sum_v[rows, :].astype(dest.dtype)


def fold_kernel(own, got, total, send1, send2, send3):
    for slot, dest in enumerate((total, send1, send2, send3)):
        dest[:, :HD] = own[slot].astype(dest.dtype)
        dest[:, HD:] = got[slot].astype(dest.dtype)


def join_kernel(side, parts_q, total, got1, got2, got3, grad_q, grad_k, grad_v):
    for head in range(2):
        sum_q = parts_q[head * GROUP].astype(F32)
        for at in range(1, GROUP):
            sum_q += parts_q[head * GROUP + at].astype(F32)
        grad_q[:, head * HD : (head + 1) * HD] = sum_q.T.astype(BF)
    sum_kv = total[...]
    for got in (got1, got2, got3):
        sum_kv += got[...].astype(F32)
    sum_kv = sum_kv.astype(BF)

    def put(first, second):
        for at, dest in enumerate((grad_k, grad_v)):
            rows = slice(at * TOK, (at + 1) * TOK)
            dest[:, :HD] = sum_kv[rows, first * HD : (first + 1) * HD]
            dest[:, HD:] = sum_kv[rows, second * HD : (second + 1) * HD]

    @pl.when(side[0] == 0)
    def _():
        put(0, 1)

    @pl.when(side[0] != 0)
    def _():
        put(1, 0)


def along(value, steps):
    pairs = []
    for at in range(RING):
        for core, shift in enumerate((steps, -steps)):
            pairs.append((2 * at + core, 2 * ((at + shift) % RING) + core))
    return lax.ppermute(value, ("z_hi", "z_lo", "core"), pairs)


def across(value):
    return lax.ppermute(value, "x_lo", [(0, 1), (1, 0)])


def body(query_rows, key_rows, value_rows, output_rows, grad_output, log_norm):
    side = lax.axis_index("x_lo").astype(jnp.int32).reshape(1)
    swap = ((4 * TOK + AUX, HD), BF)
    dout = lax.all_to_all(grad_output, ("x_hi", "y", "core", "x_lo"), 1, 0, tiled=True)
    keep, send = local(
        split_kernel,
        [swap, swap],
        side,
        *[
            pltpu.with_memory_space_constraint(rows, pltpu.HBM)
            for rows in (key_rows, value_rows, query_rows, output_rows, log_norm.T)
        ],
        far=range(1, 6),
        scratch=(pltpu.VMEM((2, TOK), F32), pltpu.SemaphoreType.DMA((9,))),
    )
    got = across(send)
    block = ((ROWS, HD), BF)
    pair = ((2 * ROWS, HD), BF)
    (keys,) = local(merge_kernel, [pair], keep, got)
    all_keys = [keys] + [along(keys, step) for step in K_STEPS]
    (pay,) = local(delta_kernel, [((PAY, HD), BF)], side, keep, got, dout)
    pays = lax.all_gather(pay, "z_hi")
    shards = ((GROUP, ROWS, HD), BF)
    parts_q, own, send = local(
        pairs_kernel,
        [((2 * GROUP, HD, TOK), BF), (shards[0], F32), shards],
        pays,
        *all_keys,
        scratch=(pltpu.VMEM((KEYS, HD), BF),) * 2 + (pltpu.VMEM((KEYS, HD), F32),) * 2,
    )
    got = across(send)
    parts_q = lax.all_to_all(parts_q, ("x_lo", "z_hi"), 0, 0, tiled=True)
    wide = ((ROWS, 2 * HD), BF)
    total, *sends = local(
        fold_kernel, [(wide[0], F32)] + [wide] * 3, own, got, cost=LONG
    )
    gots = [along(part, -step) for part, step in zip(sends, K_STEPS)]
    return tuple(
        local(join_kernel, [((TOK, 2 * HD), BF)] * 3, side, parts_q, total, *gots)
    )


def solution(mesh):
    fine = Mesh(
        mesh.devices.reshape(2, 4, 4, 2, 4, 2), ("x_lo", "z_hi", "z_lo", "x_hi", "y", "core")
    )
    blk, uly = ("x_lo", "z_hi", "z_lo"), ("x_hi", "y", "core")
    placed = P(blk, uly)
    return jax.shard_map(
        body,
        mesh=fine,
        in_specs=(placed, placed, placed, placed, P(blk + uly, None), placed),
        out_specs=(placed, placed, placed),
        check_vma=False,
    )
```
